32 devices in a mesh: seq: 8 (over z, y), head: 4 (over x, core).
Axes of the slice: x: 2, y: 2, z: 4, core: 2. Of those that a mesh axis runs over, the one named last changes fastest.
Arguments:
- queries: bfloat16 [4096, 32, 128], P('seq', 'head'), may hold values from -6 to 6
- key_matrix: bfloat16 [4096, 32, 128], P('seq', 'head'), may hold values from -6 to 6
- value_matrix: bfloat16 [4096, 32, 128], P('seq', 'head'), may hold values from -6 to 6
- level_weight: float32 [13, 32, 4096], P(None, 'head', 'seq'), may hold values from 0.25 to 4
- out_weight: bfloat16 [32, 128, 4096], P('head'), may hold values from -0.09375 to 0.09375
- grad_out: bfloat16 [4096, 4096], P('seq', 'head'), may hold values from -4 to 4
Outputs:
- mixed_out: bfloat16 [4096, 4096], P('seq', 'head')
- grad_queries: bfloat16 [4096, 32, 128], P('seq', 'head')
- grad_keys: bfloat16 [4096, 32, 128], P('seq', 'head')
- grad_values: bfloat16 [4096, 32, 128], P('seq', 'head')
- grad_levels: float32 [13, 32, 4096], P(None, 'head', 'seq')
The draws below stay inside these ranges and needn't reach their ends.
All inputs are finite; a program needn't handle non-finite values.
Results may differ from the reference program's by a relative error of at most 0.017.
Values may be sent and summed in bfloat16 or wider, within the bound.
A program may use at most 128 MiB of HBM per device.

```python
import math
import jax
import jax.numpy as jnp
from jax import lax

D = 4096
HEADS = 32
HD = 128
TOK_DEV = 512
LOCAL = 9
CROSS = 3
LEVELS = 13
TOKENS = 4096
N_HEAD = 4


def shard_levels(rng, dims, pieces, smallest, high):
    factor_of = 1.0
    for dim, blocks in pieces:
        steps = jax.random.uniform(jax.random.fold_in(jax.random.fold_in(rng, 6), dim), (blocks,), jnp.float32, smallest / len(pieces), high / len(pieces))
        factor_of = factor_of * jnp.repeat(jnp.exp(steps), dims[dim] // blocks).reshape((-1,) + (1,) * (len(dims) - 1 - dim))
    return factor_of


def bell_draw(rng, extent, deviation, reach, split=(), kind=jnp.bfloat16):
    entries = jax.random.normal(rng, extent, jnp.float32) * deviation
    if len(split) > 0:
        entries = shard_levels(rng, extent, split, -0.22, 0.18) * entries
    return jnp.clip(entries, min=-reach, max=reach).astype(kind)


def setup_inputs(seed: int = 0) -> dict:
    seeds = jax.random.split(jax.random.key(seed), 7)
    queries = bell_draw(seeds[0], (TOKENS, HEADS, HD), 1.0, 6.0, ((0, 8), (1, 4)))
    key_matrix = bell_draw(seeds[1], (TOKENS, HEADS, HD), 1.0, 6.0, ((0, 8), (1, 4)))
    value_matrix = bell_draw(seeds[2], (TOKENS, HEADS, HD), 1.0, 6.0, ((0, 8), (1, 4)))
    level_weight = jnp.clip(jnp.exp(math.log(4.0) - 2.7725887 * jax.random.uniform(seeds[3], (LEVELS, HEADS, TOKENS), jnp.float32) ** shard_levels(seeds[3], (LEVELS, HEADS, TOKENS), ((1, 4), (2, 8)), -0.2, 0.2)), 0.25, 4.0)
    out_weight = bell_draw(seeds[4], (HEADS, HD, D), (HEADS * HD) ** -0.5, 0.09375, ((0, 4),))
    grad_out = bell_draw(seeds[5], (TOKENS, D), 0.5, 4.0, ((0, 8), (1, 4)))
    return {"queries": queries, "key_matrix": key_matrix, "value_matrix": value_matrix, "level_weight": level_weight, "out_weight": out_weight, "grad_out": grad_out}


PRECISE_MATCH = lax.Precision.HIGHEST

def top_bit(differ, bit_total):
    count_bits = jnp.zeros(differ.shape, jnp.int32)
    for exponent in range(bit_total):
        count_bits = count_bits + (differ >= 2 ** exponent).astype(jnp.int32)
    return count_bits

def level_scales(level_total, head_width):
    raised = jnp.maximum(jnp.arange(level_total, dtype=jnp.int32) - 1, 0).astype(jnp.float32)
    return jnp.exp2(-0.5 * raised) / jnp.sqrt(jnp.float32(head_width))

def block_sums(packed):
    query_part, key_portion, value_portion, mix_part, weight_part = packed
    key_weighted = jnp.einsum('gpl,gpq->plq', key_portion.astype(jnp.float32), value_portion.astype(jnp.float32), precision=PRECISE_MATCH)
    far_weights = weight_part[LOCAL + 1:]
    weighted = far_weights[:, :, :, None] * jnp.transpose(query_part.astype(jnp.float32), (1, 0, 2))[None]
    back_state = jnp.einsum('jhik,ihv->jhkv', weighted, mix_part.astype(jnp.float32), precision=PRECISE_MATCH)
    return (key_weighted, back_state)

def reference(queries, key_matrix, value_matrix, level_weight, out_weight, grad_out):
    blocks_total = TOKENS // TOK_DEV
    scales = level_scales(LEVELS, HD)
    weights_all = level_weight.astype(jnp.float32) * scales[:, None, None]
    flat_out = out_weight.reshape(HEADS * HD, D)
    grad_mix = lax.dot_general(grad_out, flat_out, (((1,), (1,)), ((), ())), preferred_element_type=jnp.float32)
    grad_mix = grad_mix.astype(jnp.bfloat16).reshape(blocks_total, TOK_DEV, HEADS, HD)
    queries_b = queries.reshape(blocks_total, TOK_DEV, HEADS, HD)
    keys_b = key_matrix.reshape(blocks_total, TOK_DEV, HEADS, HD)
    values_b = value_matrix.reshape(blocks_total, TOK_DEV, HEADS, HD)
    weights_b = jnp.transpose(weights_all.reshape(LEVELS, HEADS, blocks_total, TOK_DEV), (2, 0, 1, 3))
    key_states, query_states = lax.map(block_sums, (queries_b, keys_b, values_b, grad_mix, weights_b))
    later = lax.broadcasted_iota(jnp.int32, (blocks_total, blocks_total), 0)
    earlier = lax.broadcasted_iota(jnp.int32, (blocks_total, blocks_total), 1)
    block_gap = top_bit(jnp.bitwise_xor(later, earlier), CROSS)
    level_ladder = jnp.arange(1, CROSS + 1, dtype=jnp.int32)
    masks = ((block_gap[None] == level_ladder[:, None, None]) & (earlier < later)[None]).astype(jnp.float32)
    left_states = jnp.einsum('jde,ehkv->djhkv', masks, key_states, precision=PRECISE_MATCH)
    right_states = jnp.einsum('jde,djhkv->ejhkv', masks, query_states, precision=PRECISE_MATCH)

    def block_pass(packed):
        query_part, key_portion, value_portion, mix_part, weight_part, left_part, right_part = packed
        rows_index = lax.broadcasted_iota(jnp.int32, (TOK_DEV, TOK_DEV), 0)
        cols_index = lax.broadcasted_iota(jnp.int32, (TOK_DEV, TOK_DEV), 1)
        near_gap = top_bit(jnp.bitwise_xor(rows_index, cols_index), LOCAL)
        causal = cols_index <= rows_index
        query_f = query_part.astype(jnp.float32)
        key_f = key_portion.astype(jnp.float32)
        value_f = value_portion.astype(jnp.float32)
        mix_f = mix_part.astype(jnp.float32)
        scores = jnp.einsum('ihk,jhk->hij', query_f, key_f, precision=PRECISE_MATCH)
        mixing = jnp.zeros((HEADS, TOK_DEV, TOK_DEV), jnp.float32)
        for level_now in range(LOCAL + 1):
            chosen = ((near_gap == level_now) & causal)[None]
            mixing = jnp.where(chosen, weight_part[level_now][:, :, None], mixing)
        attention = lax.optimization_barrier((scores * mixing).astype(jnp.bfloat16)).astype(jnp.float32)
        local_out = jnp.einsum('hij,jhv->ihv', attention, value_f, precision=PRECISE_MATCH)
        far_rows = jnp.transpose(weight_part[LOCAL + 1:], (0, 2, 1))[..., None]
        reads = jnp.einsum('ihk,jhkv->jihv', query_f, left_part, precision=PRECISE_MATCH)
        attended = (local_out + lax.optimization_barrier(jnp.sum(far_rows * reads, axis=0))).astype(jnp.bfloat16)
        back = jnp.einsum('ihv,jhv->hij', mix_f, value_f, precision=PRECISE_MATCH)
        product = scores * back
        near_list = []
        for level_now in range(LOCAL + 1):
            chosen = ((near_gap == level_now) & causal)[None]
            near_list.append(lax.optimization_barrier(jnp.sum(jnp.where(chosen, product, 0.0), axis=2)))
        near_grad = jnp.stack(near_list) * scales[:LOCAL + 1, None, None]
        far_grad = jnp.transpose(lax.optimization_barrier(jnp.sum(reads * mix_f[None], axis=3)), (0, 2, 1)) * scales[LOCAL + 1:, None, None]
        grad_score = lax.optimization_barrier((back * mixing).astype(jnp.bfloat16)).astype(jnp.float32)
        grad_query = jnp.einsum('hij,jhk->ihk', grad_score, key_f, precision=PRECISE_MATCH)
        grad_query = grad_query + lax.optimization_barrier(jnp.sum(far_rows * jnp.einsum('jhkv,ihv->jihk', left_part, mix_f, precision=PRECISE_MATCH), axis=0))
        grad_key = jnp.einsum('hij,ihk->jhk', grad_score, query_f, precision=PRECISE_MATCH)
        grad_key = grad_key + jnp.einsum('jhkv,ihv->ihk', right_part, value_f, precision=PRECISE_MATCH)
        grad_value = jnp.einsum('hij,ihv->jhv', attention, mix_f, precision=PRECISE_MATCH)
        grad_value = grad_value + jnp.einsum('jhkv,ihk->ihv', right_part, key_f, precision=PRECISE_MATCH)
        return (attended, grad_query.astype(jnp.bfloat16), grad_key.astype(jnp.bfloat16), grad_value.astype(jnp.bfloat16), jnp.concatenate([near_grad, far_grad], 0))
    output_rows = lax.map(block_pass, (queries_b, keys_b, values_b, grad_mix, weights_b, left_states, right_states))
    attended = output_rows[0].reshape(TOKENS, HEADS * HD)
    group_width = HEADS * HD // N_HEAD
    summed = jnp.zeros((TOKENS, D), jnp.float32)
    for group in range(N_HEAD):
        lower_row = group * group_width
        partial_sum = jnp.dot(attended[:, lower_row:lower_row + group_width], flat_out[lower_row:lower_row + group_width], preferred_element_type=jnp.float32)
        summed = summed + lax.optimization_barrier(partial_sum.astype(jnp.bfloat16)).astype(jnp.float32)
    mixed_out = summed.astype(jnp.bfloat16)
    grad_queries = output_rows[1].reshape(TOKENS, HEADS, HD)
    grad_keys = output_rows[2].reshape(TOKENS, HEADS, HD)
    grad_values = output_rows[3].reshape(TOKENS, HEADS, HD)
    grad_levels = jnp.transpose(output_rows[4], (1, 2, 0, 3)).reshape(LEVELS, HEADS, TOKENS)
    return (mixed_out, grad_queries, grad_keys, grad_values, grad_levels)
```

```python
import math

import jax
import jax.numpy as jnp
from jax import lax
from jax.experimental import pallas as pl
from jax.experimental.pallas import tpu as pltpu
from jax.sharding import PartitionSpec as P

F32 = jnp.float32
BF16 = jnp.bfloat16
TILE = 128
CHUNKS = 2


def nn(a, b):
    return jnp.dot(a, b, preferred_element_type=F32)


def nt(a, b):
    return lax.dot_general(a, b, (((1,), (1,)), ((), ())), preferred_element_type=F32)


def make_kernel(T, NH, HD, L, D, FS, n_seq, n_head):
    far = n_seq.bit_length() - 1
    near = L - far
    nx = n_head // 2
    nb = T // TILE
    H = T // 2
    R = T // CHUNKS
    tile_levels = TILE.bit_length()
    c = [2.0 ** (-max(l - 1, 0) / 2) / math.sqrt(HD) for l in range(L)]
    tri = [sum(far - i for i in range(b)) for b in range(far)]
    n_sems = 1 + 2 * (nx - 1) * CHUNKS + far + far + (nx - 1) * CHUNKS * 2 + 1

    def kernel(q_hbm, k_hbm, v_hbm, lw_hbm, w_hbm, g_hbm,
               mo, dq, dk, dv, gl,
               q, k, v, lw, w, gall, vt, qt, lev, at, mix, ds, att_t, att, acc,
               dot_, do, s_send, s_recv, s_pend, f_t, f_n, p_send, p_recv, p_pend,
               r_sum, dkl, dvl, sib_send, sib_recv, x_send, x_recv, own,
               ssem, rsem, lsem):
        sid = lax.axis_index("seq")
        hid = lax.axis_index("head")
        chip = lax.div(hid, 2)
        core = lax.rem(hid, 2)
        other = 1 - core
        sib = {"head": chip * 2 + other}

        def chip_at(d):
            return lax.rem(chip + d, nx)

        def chip_from(d):
            return lax.rem(chip + nx - d, nx)

        def bit(b):
            return lax.rem(lax.div(sid, 2**b), 2)

        def seq_peer(b):
            return {"seq": sid + 2**b * (1 - 2 * bit(b))}

        x_to = [None] + [{"head": chip_at(d) * 2 + core} for d in range(1, nx)]
        peers = [sib] + [seq_peer(b) for b in range(far)]

        used = [0]

        def remote(src, dst, dev):
            i = used[0]
            used[0] += 1
            return pltpu.make_async_remote_copy(
                src_ref=src, dst_ref=dst, send_sem=ssem.at[i], recv_sem=rsem.at[i],
                device_id=dev, device_id_type=pl.DeviceIdType.MESH,
            )

        loads = [
            pltpu.make_async_copy(a, b, lsem.at[i])
            for i, (a, b) in enumerate(
                [(k_hbm, k), (v_hbm, v), (q_hbm, q), (lw_hbm, lw), (g_hbm, gall.at[0]), (w_hbm, w)]
            )
        ]
        for copy in loads:
            copy.start()

        barrier = pltpu.get_barrier_semaphore()
        for dev in peers + x_to[1:]:
            pl.semaphore_signal(barrier, inc=1, device_id=dev, device_id_type=pl.DeviceIdType.MESH)
        pl.semaphore_wait(barrier, len(peers) + nx - 1)

        ag_x = {}
        for part in range(CHUNKS):
            rows = pl.ds(part * R, R)
            for d in range(1, nx):
                ag_x[d, part] = remote(g_hbm.at[rows], gall.at[2 * d, rows], x_to[d])
                ag_x[d, part].start()
        ag_sib = remote(g_hbm, gall.at[1], sib)
        ag_sib.start()

        loads[0].wait()
        loads[1].wait()

        def outer(h, _):
            turned = v[h].T
            vt[h] = turned
            state = nn(turned, k[h])
            s_pend[h] = state
            s_send[0, h] = state.astype(BF16)
            return 0

        lax.fori_loop(0, NH, outer, 0)
        s_copy = []
        s_copy.append(remote(s_send.at[0], s_recv.at[0], seq_peer(0)))
        s_copy[0].start()

        rows_i = lax.broadcasted_iota(jnp.int32, (TILE, TILE), 0)
        cols_i = lax.broadcasted_iota(jnp.int32, (TILE, TILE), 1)
        gap = jnp.zeros((TILE, TILE), jnp.int32)
        for e in range(tile_levels - 1):
            gap = gap + (jnp.bitwise_xor(rows_i, cols_i) >= 2**e).astype(jnp.int32)
        lev[...] = jnp.where(rows_i <= cols_i, gap, -1)

        def blank(h, _):
            for bj in range(nb):
                for bi in range(bj):
                    at[h, pl.ds(bj * TILE, TILE), pl.ds(bi * TILE, TILE)] = jnp.zeros((TILE, TILE), BF16)
            return 0

        lax.fori_loop(0, NH, blank, 0)
        for bj in range(nb):
            for bi in range(bj):
                ds[pl.ds(bj * TILE, TILE), pl.ds(bi * TILE, TILE)] = jnp.zeros((TILE, TILE), BF16)
        loads[2].wait()
        loads[3].wait()

        def weight(l, h):
            return lw[l, pl.ds(h, 1), :] * c[l]

        def block(b):
            return slice(b * TILE, (b + 1) * TILE)

        def tile_of(top, bottom, bj, bi):
            if bj * TILE < H:
                return top[block(bj), block(bi)]
            return bottom[bj * TILE - H:(bj + 1) * TILE - H, bi * TILE - H:(bi + 1) * TILE - H]

        def level_of(bj, bi):
            return (bj ^ bi).bit_length() + tile_levels - 1

        def forward(h, _):
            kh, qh = k[h], q[h]
            qt[h] = qh.T
            top = nt(kh[:H], qh)
            bottom = nt(kh[H:], qh[H:])
            ws = [weight(l, h) for l in range(near)]
            for bi in range(nb):
                m = jnp.zeros((TILE, TILE), F32)
                for l in range(tile_levels):
                    m = jnp.where(lev[...] == l, ws[l][:, block(bi)], m)
                mix[h, bi] = m
                for bj in range(bi + 1):
                    t = tile_of(top, bottom, bj, bi)
                    factor = m if bi == bj else ws[level_of(bj, bi)][:, block(bi)]
                    at[h, pl.ds(bj * TILE, TILE), pl.ds(bi * TILE, TILE)] = (t * factor).astype(BF16)
            vth = vt[h]
            att_t[h, :, :H] = nn(vth[:, :H], at[h, :H, :H])
            att_t[h, :, H:] = nn(vth, at[h, :, H:])
            return 0

        def take_state(b):
            s_copy[b].wait()
            keep = bit(b).astype(F32)

            def body(h, _):
                got = s_recv[b, h].astype(F32)
                f = got * keep
                f_t[b, h] = f.astype(BF16)
                f_n[b, h] = f.T.astype(BF16)
                if b + 1 < far:
                    total = s_pend[h] + got
                    s_pend[h] = total
                    s_send[b + 1, h] = total.astype(BF16)
                return 0

            lax.fori_loop(0, NH, body, 0)
            if b + 1 < far:
                s_copy.append(remote(s_send.at[b + 1], s_recv.at[b + 1], seq_peer(b + 1)))
                s_copy[b + 1].start()

        fwd_copy = {}

        def pass_on(part):
            rows = pl.ds(part * R, R)
            for d in range(1, nx):
                ag_x[d, part].wait_recv()
                fwd_copy[d, part] = remote(gall.at[2 * d, rows], gall.at[2 * d + 1, rows], sib)
                fwd_copy[d, part].start()

        lax.fori_loop(0, NH // 2, forward, 0)
        take_state(0)
        lax.fori_loop(NH // 2, NH, forward, 0)
        for b in range(1, far - 1):
            take_state(b)
        pass_on(0)
        loads[4].wait()
        loads[5].wait()

        MB = min(256, NH * HD)

        def add_mix(slot, src, part, first, last):
            cols = pl.ds(pl.multiple_of(src * FS, FS), FS)

            def body(i, _):
                hd = pl.ds(pl.multiple_of(i * MB, MB), MB)
                lanes = pl.ds(part * R, R)
                term = nt(w[hd, cols], gall[slot, part * R:(part + 1) * R])
                if not first:
                    term = term + acc[hd, lanes]
                acc[hd, lanes] = term
                return 0

            lax.fori_loop(0, NH * HD // MB, body, 0)

        for part in range(CHUNKS):
            add_mix(0, hid, part, True, False)
        ag_sib.wait_recv()
        for part in range(CHUNKS):
            add_mix(1, chip * 2 + other, part, False, False)
        if far > 1:
            take_state(far - 1)

        def reads(h, _):
            qth = qt[h].astype(F32)
            left = jnp.concatenate([f_t[b, h] for b in range(far)], axis=1)
            right = jnp.concatenate([(qth * weight(near + b, h)).astype(BF16) for b in range(far)], axis=0)
            total = att_t[h] + nn(left, right)
            att[:, pl.ds(pl.multiple_of(h * HD, HD), HD)] = total.T.astype(BF16)
            return 0

        lax.fori_loop(0, NH, reads, 0)

        NB = min(256, FS)

        def project(dst, slot, dest, part):
            rows = slice(part * R, (part + 1) * R)

            def body(i, _):
                lanes = pl.ds(pl.multiple_of(i * NB, NB), NB)
                cols = pl.ds(pl.multiple_of(dest * FS + i * NB, NB), NB)
                dst[slot, rows, lanes] = nn(att[rows], w[:, cols]).astype(BF16)
                return 0

            lax.fori_loop(0, FS // NB, body, 0)

        sib_copy = {}
        for part in range(CHUNKS):
            rows = pl.ds(part * R, R)
            for d in range(1, nx):
                project(sib_send, d, chip_at(d) * 2 + other, part)
                sib_copy[d, part] = remote(sib_send.at[d, rows], sib_recv.at[d, rows], sib)
                sib_copy[d, part].start()
        for part in range(1, CHUNKS):
            pass_on(part)
        x_copy = {}
        for part in range(CHUNKS):
            rows = pl.ds(part * R, R)
            for d in range(1, nx):
                project(own, d, chip_at(d) * 2 + core, part)
                sib_copy[d, part].wait_recv()
                x_send[d - 1, rows] = (own[d, rows].astype(F32) + sib_recv[d, rows].astype(F32)).astype(BF16)
                x_copy[d, part] = remote(x_send.at[d - 1, rows], x_recv.at[d - 1, rows], x_to[d])
                x_copy[d, part].start()

        for part in range(CHUNKS):
            for d in range(1, nx):
                add_mix(2 * d, chip_from(d) * 2 + core, part, False, False)
            for d in range(1, nx):
                fwd_copy[d, part].wait_recv()
                add_mix(2 * d + 1, chip_from(d) * 2 + other, part, False, False)

        def back_state(h, _):
            turned = acc[pl.ds(pl.multiple_of(h * HD, HD), HD), :]
            dot_[h] = turned.astype(BF16)
            doh = turned.T.astype(BF16)
            do[h] = doh
            qth = qt[h].astype(F32)
            for b in range(far):
                state = nn((qth * weight(near + b, h)).astype(BF16), doh)
                p_pend[b, h] = state
                p_send[b, h] = state.astype(BF16)
            return 0

        lax.fori_loop(0, NH, back_state, 0)
        p_copy = []

        def send_back(b):
            part = pl.ds(tri[b], far - b)
            p_copy.append(remote(p_send.at[part], p_recv.at[part], seq_peer(b)))
            p_copy[b].start()

        def take_back(b):
            p_copy[b].wait()
            keep = 1.0 - bit(b).astype(F32)

            def body(h, _):
                got = p_recv[tri[b], h].astype(F32) * keep
                r_sum[h] = got if b == 0 else r_sum[h] + got
                for j in range(1, far - b):
                    total = p_pend[b + j, h] + p_recv[tri[b] + j, h].astype(F32)
                    p_pend[b + j, h] = total
                    p_send[tri[b + 1] + j - 1, h] = total.astype(BF16)
                return 0

            lax.fori_loop(0, NH, body, 0)
            if b + 1 < far:
                send_back(b + 1)

        send_back(0)

        def backward(h, _):
            kh, qh, vh = k[h], q[h], v[h]
            doth, doh = dot_[h], do[h]
            s_top = nt(kh[:H], qh)
            s_bottom = nt(kh[H:], qh[H:])
            b_top = nn(vh[:H], doth)
            b_bottom = nn(vh[H:], doth[:, H:])
            ws = [weight(l, h) for l in range(near)]
            sums = [[] for _ in range(near)]
            for bi in range(nb):
                far_sums = {}
                for bj in range(bi + 1):
                    back = tile_of(b_top, b_bottom, bj, bi)
                    product = tile_of(s_top, s_bottom, bj, bi) * back
                    if bi == bj:
                        factor = mix[h, bi]
                        for l in range(tile_levels):
                            sums[l].append(
                                jnp.sum(jnp.where(lev[...] == l, product, 0.0), axis=0, keepdims=True)
                            )
                    else:
                        l = level_of(bj, bi)
                        factor = ws[l][:, block(bi)]
                        far_sums[l] = far_sums[l] + product if l in far_sums else product
                    ds[pl.ds(bj * TILE, TILE), pl.ds(bi * TILE, TILE)] = (back * factor).astype(BF16)
                for l in range(tile_levels, near):
                    if l in far_sums:
                        sums[l].append(jnp.sum(far_sums[l], axis=0, keepdims=True))
                    else:
                        sums[l].append(jnp.zeros((1, TILE), F32))
            for l in range(near):
                gl[l, pl.ds(h, 1), :] = jnp.concatenate(sums[l], axis=1) * c[l]
            dvl[h, :H] = nn(at[h, :H, :], doh)
            dvl[h, H:] = nn(at[h, H:, H:], doh[H:])
            dkl[h, :H] = nn(ds[:H, :], qh)
            dkl[h, H:] = nn(ds[H:, H:], qh[H:])
            kt = kh.T
            dqt = jnp.concatenate([nn(kt[:, :H], ds[:H, :H]), nn(kt, ds[:, H:])], axis=1)
            qth = qt[h].astype(F32)
            for b in range(far):
                u = nn(f_n[b, h], doth)
                gl[near + b, pl.ds(h, 1), :] = jnp.sum(u * qth, axis=0, keepdims=True) * c[near + b]
                dqt = dqt + u * weight(near + b, h)
            dq[h] = dqt.T.astype(BF16)
            return 0

        lax.fori_loop(0, NH // 2, backward, 0)
        take_back(0)
        lax.fori_loop(NH // 2, NH, backward, 0)
        for b in range(1, far - 1):
            take_back(b)
        for part in range(CHUNKS):
            project(sib_send, 0, chip * 2 + other, part)
        last_copy = remote(sib_send.at[0], sib_recv.at[0], sib)
        last_copy.start()
        for part in range(CHUNKS):
            project(own, 0, hid, part)
        last_copy.wait()
        for part in range(CHUNKS):
            rows = pl.ds(part * R, R)
            total = own[0, rows].astype(F32) + sib_recv[0, rows].astype(F32)
            for d in range(1, nx):
                x_copy[d, part].wait_recv()
                total = total + x_recv[d - 1, rows].astype(F32)
            mo[rows] = total.astype(BF16)
        if far > 1:
            take_back(far - 1)

        def finish(h, _):
            r = r_sum[h].astype(BF16)
            dk[h] = (dkl[h] + nt(v[h], r)).astype(BF16)
            dv[h] = (dvl[h] + nn(k[h], r)).astype(BF16)
            return 0

        lax.fori_loop(0, NH, finish, 0)
        ag_sib.wait_send()
        for group in (ag_x, fwd_copy, sib_copy, x_copy):
            for copy in group.values():
                copy.wait_send()

    tri_total = far * (far + 1) // 2
    V = pltpu.VMEM
    scratch = [
        V((NH, T, HD), BF16), V((NH, T, HD), BF16), V((NH, T, HD), BF16), V((L, NH, T), F32),
        V((NH * HD, D), BF16), V((n_head, T, FS), BF16),
        V((NH, HD, T), BF16), V((NH, HD, T), BF16), V((TILE, TILE), jnp.int32),
        V((NH, T, T), BF16), V((NH, nb, TILE, TILE), F32), V((T, T), BF16),
        V((NH, HD, T), F32), V((T, NH * HD), BF16), V((NH * HD, T), F32),
        V((NH, HD, T), BF16), V((NH, T, HD), BF16),
        V((far, NH, HD, HD), BF16), V((far, NH, HD, HD), BF16), V((NH, HD, HD), F32),
        V((far, NH, HD, HD), BF16), V((far, NH, HD, HD), BF16),
        V((tri_total, NH, HD, HD), BF16), V((tri_total, NH, HD, HD), BF16), V((far, NH, HD, HD), F32),
        V((NH, HD, HD), F32), V((NH, T, HD), F32), V((NH, T, HD), F32),
        V((nx, T, FS), BF16), V((nx, T, FS), BF16), V((nx - 1, T, FS), BF16), V((nx - 1, T, FS), BF16),
        V((nx, T, FS), BF16),
        pltpu.SemaphoreType.DMA((n_sems,)), pltpu.SemaphoreType.DMA((n_sems,)),
        pltpu.SemaphoreType.DMA((6,)),
    ]
    return kernel, scratch


def solution(mesh):
    n_seq, n_head = mesh.shape["seq"], mesh.shape["head"]

    def on_device(queries, key_matrix, value_matrix, level_weight, out_weight, grad_out):
        T, NH, HD = queries.shape
        L = level_weight.shape[0]
        D = out_weight.shape[2]
        FS = grad_out.shape[1]
        kernel, scratch = make_kernel(T, NH, HD, L, D, FS, n_seq, n_head)
        heads_first = [jnp.swapaxes(a, 0, 1) for a in (queries, key_matrix, value_matrix)]
        mo, dq, dk, dv, gl = pl.pallas_call(
            kernel,
            out_shape=(
                jax.ShapeDtypeStruct((T, FS), BF16),
                jax.ShapeDtypeStruct((NH, T, HD), BF16),
                jax.ShapeDtypeStruct((NH, T, HD), BF16),
                jax.ShapeDtypeStruct((NH, T, HD), BF16),
                jax.ShapeDtypeStruct((L, NH, T), F32),
            ),
            in_specs=[pl.BlockSpec(memory_space=pl.ANY)] * 6,
            out_specs=tuple([pl.BlockSpec(memory_space=pltpu.VMEM)] * 5),
            scratch_shapes=scratch,
            compiler_params=pltpu.CompilerParams(
                collective_id=0, has_side_effects=True, vmem_limit_bytes=62 * 1024 * 1024
            ),
        )(*heads_first, level_weight, out_weight.reshape(NH * HD, D), grad_out)
        return (mo, *[jnp.swapaxes(a, 0, 1) for a in (dq, dk, dv)], gl)

    return jax.shard_map(
        on_device,
        mesh=mesh,
        in_specs=(
            P("seq", "head", None),
            P("seq", "head", None),
            P("seq", "head", None),
            P(None, "head", "seq"),
            P("head", None, None),
            P("seq", "head"),
        ),
        out_specs=(
            P("seq", "head"),
            P("seq", "head", None),
            P("seq", "head", None),
            P("seq", "head", None),
            P(None, "head", "seq"),
        ),
        check_vma=False,
    )
```

```python
import math

import jax
import jax.numpy as jnp
from jax import lax
from jax.experimental import pallas as pl
from jax.experimental.pallas import tpu as pltpu
from jax.sharding import PartitionSpec as P

F32 = jnp.float32
BF16 = jnp.bfloat16
TILE = 128
CHUNKS = 2


def nn(a, b):
    return jnp.dot(a, b, preferred_element_type=F32)


def nt(a, b):
    return lax.dot_general(a, b, (((1,), (1,)), ((), ())), preferred_element_type=F32)


def make_kernel(T, NH, HD, L, D, FS, n_seq, n_head):
    far = n_seq.bit_length() - 1
    near = L - far
    nx = n_head // 2
    nb = T // TILE
    H = T // 2
    R = T // CHUNKS
    tile_levels = TILE.bit_length()
    c = [2.0 ** (-max(l - 1, 0) / 2) / math.sqrt(HD) for l in range(L)]
    tri = [sum(far - i for i in range(b)) for b in range(far)]
    n_sems = 1 + 2 * (nx - 1) * CHUNKS + far + far * (far + 1) // 2 + (nx - 1) * CHUNKS * 2 + 1

    def kernel(q_hbm, k_hbm, v_hbm, lw_hbm, w_hbm, g_hbm,
               mo, dq, dk, dv, gl,
               q, k, v, lw, w, gall, vt, qt, lev, at, mix, ds, att_t, att, acc,
               dot_, do, s_send, s_recv, s_pend, f_t, f_n, p_send, p_recv, p_pend,
               r_sum, dkl, dvl, sib_send, sib_recv, x_send, x_recv, own,
               raw, ssem, rsem, lsem):
        sid = lax.axis_index("seq")
        hid = lax.axis_index("head")
        chip = lax.div(hid, 2)
        core = lax.rem(hid, 2)
        other = 1 - core
        sib = {"head": chip * 2 + other}

        def chip_at(d):
            return lax.rem(chip + d, nx)

        def chip_from(d):
            return lax.rem(chip + nx - d, nx)

        def bit(b):
            return lax.rem(lax.div(sid, 2**b), 2)

        def seq_peer(b):
            return {"seq": sid + 2**b * (1 - 2 * bit(b))}

        x_to = [None] + [{"head": chip_at(d) * 2 + core} for d in range(1, nx)]
        peers = [sib] + [seq_peer(b) for b in range(far)]

        used = [0]

        def remote(src, dst, dev):
            i = used[0]
            used[0] += 1
            return pltpu.make_async_remote_copy(
                src_ref=src, dst_ref=dst, send_sem=ssem.at[i], recv_sem=rsem.at[i],
                device_id=dev, device_id_type=pl.DeviceIdType.MESH,
            )

        loads = [
            pltpu.make_async_copy(a, b, lsem.at[i])
            for i, (a, b) in enumerate(
                [(k_hbm, raw.at[0]), (v_hbm, raw.at[1]), (lw_hbm, lw), (g_hbm, gall.at[0]), (w_hbm, w), (q_hbm, raw.at[0])]
            )
        ]
        for copy in loads[:-1]:
            copy.start()

        barrier = pltpu.get_barrier_semaphore()
        for dev in peers + x_to[1:]:
            pl.semaphore_signal(barrier, inc=1, device_id=dev, device_id_type=pl.DeviceIdType.MESH)
        pl.semaphore_wait(barrier, len(peers) + nx - 1)

        ag_x = {}
        for part in range(CHUNKS):
            rows = pl.ds(part * R, R)
            for d in range(1, nx):
                ag_x[d, part] = remote(g_hbm.at[rows], gall.at[2 * d, rows], x_to[d])
                ag_x[d, part].start()
        ag_sib = remote(g_hbm, gall.at[1], sib)
        ag_sib.start()

        def by_head(slot, dst):
            def body(i, _):
                rows = pl.ds(pl.multiple_of(i * TILE, TILE), TILE)
                dst[:, rows, :] = jnp.swapaxes(raw[slot, rows], 0, 1)
                return 0

            lax.fori_loop(0, T // TILE, body, 0)

        loads[0].wait()
        by_head(0, k)
        loads[5].start()
        loads[1].wait()
        by_head(1, v)

        def outer(h, _):
            turned = v[h].T
            vt[h] = turned
            state = nn(turned, k[h])
            s_pend[h] = state
            s_send[0, h] = state.astype(BF16)
            return 0

        lax.fori_loop(0, NH, outer, 0)
        s_copy = []
        s_copy.append(remote(s_send.at[0], s_recv.at[0], seq_peer(0)))
        s_copy[0].start()

        rows_i = lax.broadcasted_iota(jnp.int32, (TILE, TILE), 0)
        cols_i = lax.broadcasted_iota(jnp.int32, (TILE, TILE), 1)
        gap = jnp.zeros((TILE, TILE), jnp.int32)
        for e in range(tile_levels - 1):
            gap = gap + (jnp.bitwise_xor(rows_i, cols_i) >= 2**e).astype(jnp.int32)
        lev[...] = jnp.where(rows_i <= cols_i, gap, -1)

        def blank(h, _):
            for bj in range(nb):
                for bi in range(bj):
                    at[h, pl.ds(bj * TILE, TILE), pl.ds(bi * TILE, TILE)] = jnp.zeros((TILE, TILE), BF16)
            return 0

        lax.fori_loop(0, NH, blank, 0)
        for bj in range(nb):
            for bi in range(bj):
                ds[pl.ds(bj * TILE, TILE), pl.ds(bi * TILE, TILE)] = jnp.zeros((TILE, TILE), BF16)
        loads[2].wait()
        loads[5].wait()
        by_head(0, q)

        def weight(l, h):
            return lw[l, pl.ds(h, 1), :] * c[l]

        def block(b):
            return slice(b * TILE, (b + 1) * TILE)

        def tile_of(top, bottom, bj, bi):
            if bj * TILE < H:
                return top[block(bj), block(bi)]
            return bottom[bj * TILE - H:(bj + 1) * TILE - H, bi * TILE - H:(bi + 1) * TILE - H]

        def level_of(bj, bi):
            return (bj ^ bi).bit_length() + tile_levels - 1

        def forward(h, _):
            kh, qh = k[h], q[h]
            qt[h] = qh.T
            top = nt(kh[:H], qh)
            bottom = nt(kh[H:], qh[H:])
            ws = [weight(l, h) for l in range(near)]
            for bi in range(nb):
                m = jnp.zeros((TILE, TILE), F32)
                for l in range(tile_levels):
                    m = jnp.where(lev[...] == l, ws[l][:, block(bi)], m)
                mix[h, bi] = m
                for bj in range(bi + 1):
                    t = tile_of(top, bottom, bj, bi)
                    factor = m if bi == bj else ws[level_of(bj, bi)][:, block(bi)]
                    at[h, pl.ds(bj * TILE, TILE), pl.ds(bi * TILE, TILE)] = (t * factor).astype(BF16)
            vth = vt[h]
            att_t[h, :, :H] = nn(vth[:, :H], at[h, :H, :H])
            att_t[h, :, H:] = nn(vth, at[h, :, H:])
            return 0

        def take_state(b):
            s_copy[b].wait()
            keep = bit(b).astype(F32)

            def body(h, _):
                got = s_recv[b, h].astype(F32)
                f = got * keep
                f_t[b, h] = f.astype(BF16)
                f_n[b, h] = f.T.astype(BF16)
                if b + 1 < far:
                    total = s_pend[h] + got
                    s_pend[h] = total
                    s_send[b + 1, h] = total.astype(BF16)
                return 0

            lax.fori_loop(0, NH, body, 0)
            if b + 1 < far:
                s_copy.append(remote(s_send.at[b + 1], s_recv.at[b + 1], seq_peer(b + 1)))
                s_copy[b + 1].start()

        fwd_copy = {}

        def pass_on(part):
            rows = pl.ds(part * R, R)
            for d in range(1, nx):
                ag_x[d, part].wait_recv()
                fwd_copy[d, part] = remote(gall.at[2 * d, rows], gall.at[2 * d + 1, rows], sib)
                fwd_copy[d, part].start()

        lax.fori_loop(0, NH // 2, forward, 0)
        take_state(0)
        lax.fori_loop(NH // 2, NH, forward, 0)
        for b in range(1, far - 1):
            take_state(b)
        pass_on(0)
        loads[3].wait()
        loads[4].wait()

        MB = min(256, NH * HD)

        def add_mix(slot, src, part, first, last):
            cols = pl.ds(pl.multiple_of(src * FS, FS), FS)

            def body(i, _):
                hd = pl.ds(pl.multiple_of(i * MB, MB), MB)
                lanes = pl.ds(part * R, R)
                term = nt(w[hd, cols], gall[slot, part * R:(part + 1) * R])
                if not first:
                    term = term + acc[hd, lanes]
                acc[hd, lanes] = term
                return 0

            lax.fori_loop(0, NH * HD // MB, body, 0)

        for part in range(CHUNKS):
            add_mix(0, hid, part, True, False)
        ag_sib.wait_recv()
        for part in range(CHUNKS):
            add_mix(1, chip * 2 + other, part, False, False)
        if far > 1:
            take_state(far - 1)

        def reads(h, _):
            qth = qt[h].astype(F32)
            left = jnp.concatenate([f_t[b, h] for b in range(far)], axis=1)
            right = jnp.concatenate([(qth * weight(near + b, h)).astype(BF16) for b in range(far)], axis=0)
            total = att_t[h] + nn(left, right)
            att[:, pl.ds(pl.multiple_of(h * HD, HD), HD)] = total.T.astype(BF16)
            return 0

        lax.fori_loop(0, NH, reads, 0)

        NB = min(256, FS)

        def project(dst, slot, dest, part):
            rows = slice(part * R, (part + 1) * R)

            def body(i, _):
                lanes = pl.ds(pl.multiple_of(i * NB, NB), NB)
                cols = pl.ds(pl.multiple_of(dest * FS + i * NB, NB), NB)
                dst[slot, rows, lanes] = nn(att[rows], w[:, cols]).astype(BF16)
                return 0

            lax.fori_loop(0, FS // NB, body, 0)

        sib_copy = {}
        for part in range(CHUNKS):
            rows = pl.ds(part * R, R)
            for d in range(1, nx):
                project(sib_send, d, chip_at(d) * 2 + other, part)
                sib_copy[d, part] = remote(sib_send.at[d, rows], sib_recv.at[d, rows], sib)
                sib_copy[d, part].start()
        for part in range(1, CHUNKS):
            pass_on(part)
        x_copy = {}
        for part in range(CHUNKS):
            rows = pl.ds(part * R, R)
            for d in range(1, nx):
                project(own, d, chip_at(d) * 2 + core, part)
                sib_copy[d, part].wait_recv()
                x_send[d - 1, rows] = (own[d, rows].astype(F32) + sib_recv[d, rows].astype(F32)).astype(BF16)
                x_copy[d, part] = remote(x_send.at[d - 1, rows], x_recv.at[d - 1, rows], x_to[d])
                x_copy[d, part].start()

        for part in range(CHUNKS):
            for d in range(1, nx):
                add_mix(2 * d, chip_from(d) * 2 + core, part, False, False)
            for d in range(1, nx):
                fwd_copy[d, part].wait_recv()
                add_mix(2 * d + 1, chip_from(d) * 2 + other, part, False, False)

        def mix_grad(h, _):
            turned = acc[pl.ds(pl.multiple_of(h * HD, HD), HD), :]
            dot_[h] = turned.astype(BF16)
            do[h] = turned.T.astype(BF16)
            return 0

        lax.fori_loop(0, NH, mix_grad, 0)
        p_copy = {}

        def send_back(j, b):
            i = tri[b] + j - b
            p_copy[j, b] = remote(p_send.at[i], p_recv.at[i], seq_peer(b))
            p_copy[j, b].start()

        for j in reversed(range(far)):

            def back_state(h, _):
                scaled = (qt[h].astype(F32) * weight(near + j, h)).astype(BF16)
                state = nn(scaled, do[h])
                p_pend[j, h] = state
                p_send[j, h] = state.astype(BF16)
                return 0

            lax.fori_loop(0, NH, back_state, 0)
            send_back(j, 0)

        started = []

        def take_back(j, b):
            p_copy[j, b].wait()
            keep = 1.0 - bit(b).astype(F32)

            def body(h, _):
                got = p_recv[tri[b] + j - b, h].astype(F32)
                if b < j:
                    total = p_pend[j, h] + got
                    p_pend[j, h] = total
                    p_send[tri[b + 1] + j - b - 1, h] = total.astype(BF16)
                elif started:
                    r_sum[h] = r_sum[h] + got * keep
                else:
                    r_sum[h] = got * keep
                return 0

            lax.fori_loop(0, NH, body, 0)
            if b < j:
                send_back(j, b + 1)
            else:
                started.append(j)

        def backward(h, _):
            kh, qh, vh = k[h], q[h], v[h]
            doth, doh = dot_[h], do[h]
            s_top = nt(kh[:H], qh)
            s_bottom = nt(kh[H:], qh[H:])
            b_top = nn(vh[:H], doth)
            b_bottom = nn(vh[H:], doth[:, H:])
            ws = [weight(l, h) for l in range(near)]
            sums = [[] for _ in range(near)]
            for bi in range(nb):
                far_sums = {}
                for bj in range(bi + 1):
                    back = tile_of(b_top, b_bottom, bj, bi)
                    product = tile_of(s_top, s_bottom, bj, bi) * back
                    if bi == bj:
                        factor = mix[h, bi]
                        for l in range(tile_levels):
                            sums[l].append(
                                jnp.sum(jnp.where(lev[...] == l, product, 0.0), axis=0, keepdims=True)
                            )
                    else:
                        l = level_of(bj, bi)
                        factor = ws[l][:, block(bi)]
                        far_sums[l] = far_sums[l] + product if l in far_sums else product
                    ds[pl.ds(bj * TILE, TILE), pl.ds(bi * TILE, TILE)] = (back * factor).astype(BF16)
                for l in range(tile_levels, near):
                    if l in far_sums:
                        sums[l].append(jnp.sum(far_sums[l], axis=0, keepdims=True))
                    else:
                        sums[l].append(jnp.zeros((1, TILE), F32))
            for l in range(near):
                gl[l, pl.ds(h, 1), :] = jnp.concatenate(sums[l], axis=1) * c[l]
            dvl[h, :H] = nn(at[h, :H, :], doh)
            dvl[h, H:] = nn(at[h, H:, H:], doh[H:])
            dkl[h, :H] = nn(ds[:H, :], qh)
            dkl[h, H:] = nn(ds[H:, H:], qh[H:])
            kt = kh.T
            dqt = jnp.concatenate([nn(kt[:, :H], ds[:H, :H]), nn(kt, ds[:, H:])], axis=1)
            qth = qt[h].astype(F32)
            for b in range(far):
                u = nn(f_n[b, h], doth)
                gl[near + b, pl.ds(h, 1), :] = jnp.sum(u * qth, axis=0, keepdims=True) * c[near + b]
                dqt = dqt + u * weight(near + b, h)
            dq[h] = dqt.T.astype(BF16)
            return 0

        arrivals = [(j, b) for b in range(far) for j in reversed(range(b, far))]
        early = [a for a in arrivals if a[1] == 0]
        late = [a for a in arrivals if a[1] == far - 1]
        cuts = [0, (3 * NH) // 8, (6 * NH) // 8, NH]
        lax.fori_loop(cuts[0], cuts[1], backward, 0)
        for j, b in early:
            take_back(j, b)
        lax.fori_loop(cuts[1], cuts[2], backward, 0)
        for j, b in arrivals:
            if (j, b) not in early and (j, b) not in late:
                take_back(j, b)
        lax.fori_loop(cuts[2], cuts[3], backward, 0)
        for part in range(CHUNKS):
            project(sib_send, 0, chip * 2 + other, part)
        last_copy = remote(sib_send.at[0], sib_recv.at[0], sib)
        last_copy.start()
        for part in range(CHUNKS):
            project(own, 0, hid, part)
        last_copy.wait()
        for part in range(CHUNKS):
            rows = pl.ds(part * R, R)
            total = own[0, rows].astype(F32) + sib_recv[0, rows].astype(F32)
            for d in range(1, nx):
                x_copy[d, part].wait_recv()
                total = total + x_recv[d - 1, rows].astype(F32)
            mo[rows] = total.astype(BF16)
        for j, b in late:
            if b > 0:
                take_back(j, b)

        def finish(h, _):
            r = r_sum[h].astype(BF16)
            dk[h] = (dkl[h] + nt(v[h], r)).astype(BF16)
            dv[h] = (dvl[h] + nn(k[h], r)).astype(BF16)
            return 0

        lax.fori_loop(0, NH, finish, 0)
        ag_sib.wait_send()
        for group in (ag_x, fwd_copy, sib_copy, x_copy):
            for copy in group.values():
                copy.wait_send()

    tri_total = far * (far + 1) // 2
    V = pltpu.VMEM
    scratch = [
        V((NH, T, HD), BF16), V((NH, T, HD), BF16), V((NH, T, HD), BF16), V((L, NH, T), F32),
        V((NH * HD, D), BF16), V((n_head, T, FS), BF16),
        V((NH, HD, T), BF16), V((NH, HD, T), BF16), V((TILE, TILE), jnp.int32),
        V((NH, T, T), BF16), V((NH, nb, TILE, TILE), F32), V((T, T), BF16),
        V((NH, HD, T), F32), V((T, NH * HD), BF16), V((NH * HD, T), F32),
        V((NH, HD, T), BF16), V((NH, T, HD), BF16),
        V((far, NH, HD, HD), BF16), V((far, NH, HD, HD), BF16), V((NH, HD, HD), F32),
        V((far, NH, HD, HD), BF16), V((far, NH, HD, HD), BF16),
        V((tri_total, NH, HD, HD), BF16), V((tri_total, NH, HD, HD), BF16), V((far, NH, HD, HD), F32),
        V((NH, HD, HD), F32), V((NH, T, HD), F32), V((NH, T, HD), F32),
        V((nx, T, FS), BF16), V((nx, T, FS), BF16), V((nx - 1, T, FS), BF16), V((nx - 1, T, FS), BF16),
        V((nx, T, FS), BF16), V((2, T, NH, HD), BF16),
        pltpu.SemaphoreType.DMA((n_sems,)), pltpu.SemaphoreType.DMA((n_sems,)),
        pltpu.SemaphoreType.DMA((6,)),
    ]
    return kernel, scratch


def lay_out_kernel(mo, dq, dk, dv, gl, mo_out, dq_out, dk_out, dv_out, gl_out):
    mo_out[...] = mo[...]
    for a, b in ((dq, dq_out), (dk, dk_out), (dv, dv_out)):
        b[...] = jnp.swapaxes(a[...], 0, 1)
    gl_out[...] = gl[...]


def lay_out(results, T, NH, HD, L, FS):
    heads = pl.BlockSpec((NH, TILE, HD), lambda i: (0, i, 0))
    tokens = pl.BlockSpec((TILE, NH, HD), lambda i: (i, 0, 0))
    flat = pl.BlockSpec((TILE, FS), lambda i: (i, 0))
    levels = pl.BlockSpec((L, NH, TILE), lambda i: (0, 0, i))
    return pl.pallas_call(
        lay_out_kernel,
        grid=(T // TILE,),
        out_shape=(
            jax.ShapeDtypeStruct((T, FS), BF16),
            jax.ShapeDtypeStruct((T, NH, HD), BF16),
            jax.ShapeDtypeStruct((T, NH, HD), BF16),
            jax.ShapeDtypeStruct((T, NH, HD), BF16),
            jax.ShapeDtypeStruct((L, NH, T), F32),
        ),
        in_specs=[flat, heads, heads, heads, levels],
        out_specs=(flat, tokens, tokens, tokens, levels),
    )(*results)


def solution(mesh):
    n_seq, n_head = mesh.shape["seq"], mesh.shape["head"]

    def on_device(queries, key_matrix, value_matrix, level_weight, out_weight, grad_out):
        T, NH, HD = queries.shape
        L = level_weight.shape[0]
        D = out_weight.shape[2]
        FS = grad_out.shape[1]
        kernel, scratch = make_kernel(T, NH, HD, L, D, FS, n_seq, n_head)
        results = pl.pallas_call(
            kernel,
            out_shape=(
                jax.ShapeDtypeStruct((T, FS), BF16),
                jax.ShapeDtypeStruct((NH, T, HD), BF16),
                jax.ShapeDtypeStruct((NH, T, HD), BF16),
                jax.ShapeDtypeStruct((NH, T, HD), BF16),
                jax.ShapeDtypeStruct((L, NH, T), F32),
            ),
            in_specs=[pl.BlockSpec(memory_space=pl.ANY)] * 6,
            out_specs=tuple([pl.BlockSpec(memory_space=pltpu.VMEM)] * 5),
            scratch_shapes=scratch,
            compiler_params=pltpu.CompilerParams(
                collective_id=0, has_side_effects=True, vmem_limit_bytes=62 * 1024 * 1024
            ),
        )(queries, key_matrix, value_matrix, level_weight, out_weight.reshape(NH * HD, D), grad_out)
        return lay_out(results, T, NH, HD, L, FS)

    return jax.shard_map(
        on_device,
        mesh=mesh,
        in_specs=(
            P("seq", "head", None),
            P("seq", "head", None),
            P("seq", "head", None),
            P(None, "head", "seq"),
            P("head", None, None),
            P("seq", "head"),
        ),
        out_specs=(
            P("seq", "head"),
            P("seq", "head", None),
            P("seq", "head", None),
            P("seq", "head", None),
            P(None, "head", "seq"),
        ),
        check_vma=False,
    )
```

```python
import math

import jax
import jax.numpy as jnp
from jax import lax
from jax.experimental import pallas as pl
from jax.experimental.pallas import tpu as pltpu
from jax.sharding import PartitionSpec as P

F32 = jnp.float32
BF16 = jnp.bfloat16
TILE = 128
CHUNKS = 2


def nn(a, b):
    return jnp.dot(a, b, preferred_element_type=F32)


def nt(a, b):
    return lax.dot_general(a, b, (((1,), (1,)), ((), ())), preferred_element_type=F32)


def make_kernel(T, NH, HD, L, D, FS, n_seq, n_head):
    far = n_seq.bit_length() - 1
    near = L - far
    nx = n_head // 2
    nb = T // TILE
    H = T // 2
    R = T // CHUNKS
    tile_levels = TILE.bit_length()
    c = [2.0 ** (-max(l - 1, 0) / 2) / math.sqrt(HD) for l in range(L)]
    n_sems = 1 + 2 * (nx - 1) * CHUNKS + far + far * (2 * far) + (nx - 1) * CHUNKS * 2 + 1

    def kernel(q_hbm, k_hbm, v_hbm, lw_hbm, w_hbm, g_hbm,
               mo, dq, dk, dv, gl,
               q, k, v, lw, w, gall, vt, qt, lev, at, mix, ds, att_t, att, acc,
               dot_, do, s_send, s_recv, s_pend, f_t, f_n, p_send, p_recv, p_pend,
               p_done, dkl, dvl, sib_send, sib_recv, x_send, x_recv, own,
               raw, ssem, rsem, lsem):
        sid = lax.axis_index("seq")
        hid = lax.axis_index("head")
        chip = lax.div(hid, 2)
        core = lax.rem(hid, 2)
        other = 1 - core
        sib = {"head": chip * 2 + other}

        def chip_at(d):
            return lax.rem(chip + d, nx)

        def chip_from(d):
            return lax.rem(chip + nx - d, nx)

        def bit(b):
            return lax.rem(lax.div(sid, 2**b), 2)

        def seq_peer(b):
            return {"seq": sid + 2**b * (1 - 2 * bit(b))}

        x_to = [None] + [{"head": chip_at(d) * 2 + core} for d in range(1, nx)]
        peers = [sib] + [seq_peer(b) for b in range(far)]

        used = [0]

        def remote(src, dst, dev):
            i = used[0]
            used[0] += 1
            return pltpu.make_async_remote_copy(
                src_ref=src, dst_ref=dst, send_sem=ssem.at[i], recv_sem=rsem.at[i],
                device_id=dev, device_id_type=pl.DeviceIdType.MESH,
            )

        loads = [
            pltpu.make_async_copy(a, b, lsem.at[i])
            for i, (a, b) in enumerate(
                [(k_hbm, raw.at[0]), (v_hbm, raw.at[1]), (lw_hbm, lw), (g_hbm, gall.at[0]), (w_hbm, w), (q_hbm, raw.at[0])]
            )
        ]
        for copy in loads[:-1]:
            copy.start()

        barrier = pltpu.get_barrier_semaphore()
        for dev in peers + x_to[1:]:
            pl.semaphore_signal(barrier, inc=1, device_id=dev, device_id_type=pl.DeviceIdType.MESH)
        pl.semaphore_wait(barrier, len(peers) + nx - 1)

        ag_x = {}
        for part in range(CHUNKS):
            rows = pl.ds(part * R, R)
            for d in range(1, nx):
                ag_x[d, part] = remote(g_hbm.at[rows], gall.at[2 * d, rows], x_to[d])
                ag_x[d, part].start()
        ag_sib = remote(g_hbm, gall.at[1], sib)
        ag_sib.start()

        def by_head(slot, dst):
            def body(i, _):
                rows = pl.ds(pl.multiple_of(i * TILE, TILE), TILE)
                dst[:, rows, :] = jnp.swapaxes(raw[slot, rows], 0, 1)
                return 0

            lax.fori_loop(0, T // TILE, body, 0)

        loads[0].wait()
        by_head(0, k)
        loads[5].start()
        loads[1].wait()
        by_head(1, v)

        def outer(h, _):
            turned = v[h].T
            vt[h] = turned
            state = nn(turned, k[h])
            s_pend[h] = state
            s_send[0, h] = state.astype(BF16)
            return 0

        lax.fori_loop(0, NH, outer, 0)
        s_copy = []
        s_copy.append(remote(s_send.at[0], s_recv.at[0], seq_peer(0)))
        s_copy[0].start()

        rows_i = lax.broadcasted_iota(jnp.int32, (TILE, TILE), 0)
        cols_i = lax.broadcasted_iota(jnp.int32, (TILE, TILE), 1)
        gap = jnp.zeros((TILE, TILE), jnp.int32)
        for e in range(tile_levels - 1):
            gap = gap + (jnp.bitwise_xor(rows_i, cols_i) >= 2**e).astype(jnp.int32)
        lev[...] = jnp.where(rows_i <= cols_i, gap, -1)

        def blank(h, _):
            for bj in range(nb):
                for bi in range(bj):
                    at[h, pl.ds(bj * TILE, TILE), pl.ds(bi * TILE, TILE)] = jnp.zeros((TILE, TILE), BF16)
            return 0

        lax.fori_loop(0, NH, blank, 0)
        for bj in range(nb):
            for bi in range(bj):
                ds[pl.ds(bj * TILE, TILE), pl.ds(bi * TILE, TILE)] = jnp.zeros((TILE, TILE), BF16)
        loads[2].wait()
        loads[5].wait()
        by_head(0, q)

        def weight(l, h):
            return lw[l, pl.ds(h, 1), :] * c[l]

        def block(b):
            return slice(b * TILE, (b + 1) * TILE)

        def tile_of(top, bottom, bj, bi):
            if bj * TILE < H:
                return top[block(bj), block(bi)]
            return bottom[bj * TILE - H:(bj + 1) * TILE - H, bi * TILE - H:(bi + 1) * TILE - H]

        def level_of(bj, bi):
            return (bj ^ bi).bit_length() + tile_levels - 1

        def forward(h, _):
            kh, qh = k[h], q[h]
            qt[h] = qh.T
            top = nt(kh[:H], qh)
            bottom = nt(kh[H:], qh[H:])
            ws = [weight(l, h) for l in range(near)]
            for bi in range(nb):
                m = jnp.zeros((TILE, TILE), F32)
                for l in range(tile_levels):
                    m = jnp.where(lev[...] == l, ws[l][:, block(bi)], m)
                mix[h, bi] = m
                for bj in range(bi + 1):
                    t = tile_of(top, bottom, bj, bi)
                    factor = m if bi == bj else ws[level_of(bj, bi)][:, block(bi)]
                    at[h, pl.ds(bj * TILE, TILE), pl.ds(bi * TILE, TILE)] = (t * factor).astype(BF16)
            vth = vt[h]
            att_t[h, :, :H] = nn(vth[:, :H], at[h, :H, :H])
            att_t[h, :, H:] = nn(vth, at[h, :, H:])
            return 0

        def take_state(b):
            s_copy[b].wait()
            keep = bit(b).astype(F32)

            def body(h, _):
                got = s_recv[b, h].astype(F32)
                f = got * keep
                f_t[b, h] = f.astype(BF16)
                f_n[b, h] = f.T.astype(BF16)
                if b + 1 < far:
                    total = s_pend[h] + got
                    s_pend[h] = total
                    s_send[b + 1, h] = total.astype(BF16)
                return 0

            lax.fori_loop(0, NH, body, 0)
            if b + 1 < far:
                s_copy.append(remote(s_send.at[b + 1], s_recv.at[b + 1], seq_peer(b + 1)))
                s_copy[b + 1].start()

        fwd_copy = {}

        def pass_on(part):
            rows = pl.ds(part * R, R)
            for d in range(1, nx):
                ag_x[d, part].wait_recv()
                fwd_copy[d, part] = remote(gall.at[2 * d, rows], gall.at[2 * d + 1, rows], sib)
                fwd_copy[d, part].start()

        lax.fori_loop(0, NH // 2, forward, 0)
        take_state(0)
        lax.fori_loop(NH // 2, NH, forward, 0)
        for b in range(1, far - 1):
            take_state(b)
        pass_on(0)
        loads[3].wait()
        loads[4].wait()

        MB = min(256, NH * HD)

        def add_mix(slot, src, part, first, last):
            cols = pl.ds(pl.multiple_of(src * FS, FS), FS)

            def body(i, _):
                hd = pl.ds(pl.multiple_of(i * MB, MB), MB)
                lanes = pl.ds(part * R, R)
                term = nt(w[hd, cols], gall[slot, part * R:(part + 1) * R])
                if not first:
                    term = term + acc[hd, lanes]
                acc[hd, lanes] = term
                return 0

            lax.fori_loop(0, NH * HD // MB, body, 0)

        for part in range(CHUNKS):
            add_mix(0, hid, part, True, False)
        ag_sib.wait_recv()
        for part in range(CHUNKS):
            add_mix(1, chip * 2 + other, part, False, False)
        for part in range(CHUNKS):
            if part > 0:
                pass_on(part)
            for d in range(1, nx):
                add_mix(2 * d, chip_from(d) * 2 + core, part, False, False)
            for d in range(1, nx):
                fwd_copy[d, part].wait_recv()
                add_mix(2 * d + 1, chip_from(d) * 2 + other, part, False, False)

        def mix_grad(h, _):
            turned = acc[pl.ds(pl.multiple_of(h * HD, HD), HD), :]
            dot_[h] = turned.astype(BF16)
            do[h] = turned.T.astype(BF16)
            return 0

        lax.fori_loop(0, NH, mix_grad, 0)
        slots = [0]

        def start_chain(j):
            plan, count = [], NH
            for b in range(j):
                split = count % 2 == 0
                plan.append((b, "sum", split))
                count = count // 2 if split else count
            plan.append((j, "last", False))
            plan += [(b, "join", True) for b, _, split in reversed(plan[:-1]) if split]
            return {"level": j, "plan": plan, "at": 0, "offset": sid * 0, "count": NH}

        def send(chain):
            j = chain["level"]
            b, kind, split = chain["plan"][chain["at"]]
            offset, count = chain["offset"], chain["count"]
            if kind == "join":
                part = pl.ds(offset, count)
                copy = remote(p_done.at[j, part], p_done.at[j, part], seq_peer(b))
            else:
                half = count // 2 if split else count
                first = offset + (1 - bit(b)) * half if split else offset
                slot = slots[0]
                slots[0] += half

                def fill(i, _):
                    p_send[slot + i] = p_pend[j, first + i].astype(BF16)
                    return 0

                lax.fori_loop(0, half, fill, 0)
                source = p_send.at[pl.ds(slot, half)]
                if kind == "last":
                    copy = remote(source, p_done.at[j, pl.ds(offset, count)], seq_peer(b))
                else:
                    copy = remote(source, p_recv.at[pl.ds(slot, half)], seq_peer(b))
                    chain["offset"] = offset + bit(b) * half if split else offset
                    chain["count"] = half
                    chain["slot"] = slot
            copy.start()
            chain["copy"] = copy

        def advance(chain):
            j = chain["level"]
            b, kind, split = chain["plan"][chain["at"]]
            chain["copy"].wait()
            if kind == "sum":
                slot, offset = chain["slot"], chain["offset"]

                def add(i, _):
                    p_pend[j, offset + i] = p_pend[j, offset + i] + p_recv[slot + i].astype(F32)
                    return 0

                lax.fori_loop(0, chain["count"], add, 0)
            elif kind == "join":
                chain["offset"] = chain["offset"] - bit(b) * chain["count"]
                chain["count"] *= 2
            chain["at"] += 1
            if chain["at"] < len(chain["plan"]):
                send(chain)

        chains = []
        for j in reversed(range(far)):

            def back_state(h, _):
                scaled = (qt[h].astype(F32) * weight(near + j, h)).astype(BF16)
                p_pend[j, h] = nn(scaled, do[h])
                return 0

            lax.fori_loop(0, NH, back_state, 0)
            chains.append(start_chain(j))
            send(chains[-1])

        def poll():
            for chain in chains:
                if chain["at"] < len(chain["plan"]):
                    advance(chain)

        if far > 1:
            take_state(far - 1)

        def reads(h, _):
            qth = qt[h].astype(F32)
            left = jnp.concatenate([f_t[b, h] for b in range(far)], axis=1)
            right = jnp.concatenate([(qth * weight(near + b, h)).astype(BF16) for b in range(far)], axis=0)
            total = att_t[h] + nn(left, right)
            att[:, pl.ds(pl.multiple_of(h * HD, HD), HD)] = total.T.astype(BF16)
            return 0

        lax.fori_loop(0, NH, reads, 0)

        NB = min(256, FS)

        def project(dst, slot, dest, part):
            rows = slice(part * R, (part + 1) * R)

            def body(i, _):
                lanes = pl.ds(pl.multiple_of(i * NB, NB), NB)
                cols = pl.ds(pl.multiple_of(dest * FS + i * NB, NB), NB)
                dst[slot, rows, lanes] = nn(att[rows], w[:, cols]).astype(BF16)
                return 0

            lax.fori_loop(0, FS // NB, body, 0)

        sib_copy = {}
        for part in range(CHUNKS):
            rows = pl.ds(part * R, R)
            for d in range(1, nx):
                project(sib_send, d, chip_at(d) * 2 + other, part)
                sib_copy[d, part] = remote(sib_send.at[d, rows], sib_recv.at[d, rows], sib)
                sib_copy[d, part].start()
        poll()
        x_copy = {}
        for part in range(CHUNKS):
            rows = pl.ds(part * R, R)
            for d in range(1, nx):
                project(own, d, chip_at(d) * 2 + core, part)
                sib_copy[d, part].wait_recv()
                x_send[d - 1, rows] = (own[d, rows].astype(F32) + sib_recv[d, rows].astype(F32)).astype(BF16)
                x_copy[d, part] = remote(x_send.at[d - 1, rows], x_recv.at[d - 1, rows], x_to[d])
                x_copy[d, part].start()

        poll()

        def backward(h, _):
            kh, qh, vh = k[h], q[h], v[h]
            doth, doh = dot_[h], do[h]
            s_top = nt(kh[:H], qh)
            s_bottom = nt(kh[H:], qh[H:])
            b_top = nn(vh[:H], doth)
            b_bottom = nn(vh[H:], doth[:, H:])
            ws = [weight(l, h) for l in range(near)]
            sums = [[] for _ in range(near)]
            for bi in range(nb):
                far_sums = {}
                for bj in range(bi + 1):
                    back = tile_of(b_top, b_bottom, bj, bi)
                    product = tile_of(s_top, s_bottom, bj, bi) * back
                    if bi == bj:
                        factor = mix[h, bi]
                        for l in range(tile_levels):
                            sums[l].append(
                                jnp.sum(jnp.where(lev[...] == l, product, 0.0), axis=0, keepdims=True)
                            )
                    else:
                        l = level_of(bj, bi)
                        factor = ws[l][:, block(bi)]
                        far_sums[l] = far_sums[l] + product if l in far_sums else product
                    ds[pl.ds(bj * TILE, TILE), pl.ds(bi * TILE, TILE)] = (back * factor).astype(BF16)
                for l in range(tile_levels, near):
                    if l in far_sums:
                        sums[l].append(jnp.sum(far_sums[l], axis=0, keepdims=True))
                    else:
                        sums[l].append(jnp.zeros((1, TILE), F32))
            for l in range(near):
                gl[l, pl.ds(h, 1), :] = jnp.concatenate(sums[l], axis=1) * c[l]
            dvl[h, :H] = nn(at[h, :H, :], doh)
            dvl[h, H:] = nn(at[h, H:, H:], doh[H:])
            dkl[h, :H] = nn(ds[:H, :], qh)
            dkl[h, H:] = nn(ds[H:, H:], qh[H:])
            kt = kh.T
            dqt = jnp.concatenate([nn(kt[:, :H], ds[:H, :H]), nn(kt, ds[:, H:])], axis=1)
            qth = qt[h].astype(F32)
            for b in range(far):
                u = nn(f_n[b, h], doth)
                gl[near + b, pl.ds(h, 1), :] = jnp.sum(u * qth, axis=0, keepdims=True) * c[near + b]
                dqt = dqt + u * weight(near + b, h)
            dq[h] = dqt.T.astype(BF16)
            return 0

        cuts = [0, (3 * NH) // 8, (6 * NH) // 8, NH]
        lax.fori_loop(cuts[0], cuts[1], backward, 0)
        poll()
        lax.fori_loop(cuts[1], cuts[2], backward, 0)
        poll()
        for part in range(CHUNKS):
            project(sib_send, 0, chip * 2 + other, part)
        last_copy = remote(sib_send.at[0], sib_recv.at[0], sib)
        last_copy.start()
        for part in range(CHUNKS):
            project(own, 0, hid, part)
        lax.fori_loop(cuts[2], cuts[3], backward, 0)
        for _ in range(max(2 * far - 1 - 4, 0)):
            poll()

        def finish(h, _):
            r = sum(p_done[j, h].astype(F32) * (1.0 - bit(j).astype(F32)) for j in range(far)).astype(BF16)
            dk[h] = (dkl[h] + nt(v[h], r)).astype(BF16)
            dv[h] = (dvl[h] + nn(k[h], r)).astype(BF16)
            return 0

        lax.fori_loop(0, NH, finish, 0)
        last_copy.wait()
        for part in range(CHUNKS):
            rows = pl.ds(part * R, R)
            total = own[0, rows].astype(F32) + sib_recv[0, rows].astype(F32)
            for d in range(1, nx):
                x_copy[d, part].wait_recv()
                total = total + x_recv[d - 1, rows].astype(F32)
            mo[rows] = total.astype(BF16)
        ag_sib.wait_send()
        for group in (ag_x, fwd_copy, sib_copy, x_copy):
            for copy in group.values():
                copy.wait_send()

    slots_total = 0
    for j in range(far):
        count = NH
        for _ in range(j):
            count = count // 2 if count % 2 == 0 else count
            slots_total += count
        slots_total += count
    V = pltpu.VMEM
    scratch = [
        V((NH, T, HD), BF16), V((NH, T, HD), BF16), V((NH, T, HD), BF16), V((L, NH, T), F32),
        V((NH * HD, D), BF16), V((n_head, T, FS), BF16),
        V((NH, HD, T), BF16), V((NH, HD, T), BF16), V((TILE, TILE), jnp.int32),
        V((NH, T, T), BF16), V((NH, nb, TILE, TILE), F32), V((T, T), BF16),
        V((NH, HD, T), F32), V((T, NH * HD), BF16), V((NH * HD, T), F32),
        V((NH, HD, T), BF16), V((NH, T, HD), BF16),
        V((far, NH, HD, HD), BF16), V((far, NH, HD, HD), BF16), V((NH, HD, HD), F32),
        V((far, NH, HD, HD), BF16), V((far, NH, HD, HD), BF16),
        V((slots_total, HD, HD), BF16), V((slots_total, HD, HD), BF16), V((far, NH, HD, HD), F32),
        V((far, NH, HD, HD), BF16), V((NH, T, HD), F32), V((NH, T, HD), F32),
        V((nx, T, FS), BF16), V((nx, T, FS), BF16), V((nx - 1, T, FS), BF16), V((nx - 1, T, FS), BF16),
        V((nx, T, FS), BF16), V((2, T, NH, HD), BF16),
        pltpu.SemaphoreType.DMA((n_sems,)), pltpu.SemaphoreType.DMA((n_sems,)),
        pltpu.SemaphoreType.DMA((6,)),
    ]
    return kernel, scratch


def lay_out_kernel(mo, dq, dk, dv, gl, mo_out, dq_out, dk_out, dv_out, gl_out):
    mo_out[...] = mo[...]
    for a, b in ((dq, dq_out), (dk, dk_out), (dv, dv_out)):
        b[...] = jnp.swapaxes(a[...], 0, 1)
    gl_out[...] = gl[...]


def lay_out(results, T, NH, HD, L, FS):
    heads = pl.BlockSpec((NH, TILE, HD), lambda i: (0, i, 0))
    tokens = pl.BlockSpec((TILE, NH, HD), lambda i: (i, 0, 0))
    flat = pl.BlockSpec((TILE, FS), lambda i: (i, 0))
    levels = pl.BlockSpec((L, NH, TILE), lambda i: (0, 0, i))
    return pl.pallas_call(
        lay_out_kernel,
        grid=(T // TILE,),
        out_shape=(
            jax.ShapeDtypeStruct((T, FS), BF16),
            jax.ShapeDtypeStruct((T, NH, HD), BF16),
            jax.ShapeDtypeStruct((T, NH, HD), BF16),
            jax.ShapeDtypeStruct((T, NH, HD), BF16),
            jax.ShapeDtypeStruct((L, NH, T), F32),
        ),
        in_specs=[flat, heads, heads, heads, levels],
        out_specs=(flat, tokens, tokens, tokens, levels),
    )(*results)


def solution(mesh):
    n_seq, n_head = mesh.shape["seq"], mesh.shape["head"]

    def on_device(queries, key_matrix, value_matrix, level_weight, out_weight, grad_out):
        T, NH, HD = queries.shape
        L = level_weight.shape[0]
        D = out_weight.shape[2]
        FS = grad_out.shape[1]
        kernel, scratch = make_kernel(T, NH, HD, L, D, FS, n_seq, n_head)
        results = pl.pallas_call(
            kernel,
            out_shape=(
                jax.ShapeDtypeStruct((T, FS), BF16),
                jax.ShapeDtypeStruct((NH, T, HD), BF16),
                jax.ShapeDtypeStruct((NH, T, HD), BF16),
                jax.ShapeDtypeStruct((NH, T, HD), BF16),
                jax.ShapeDtypeStruct((L, NH, T), F32),
            ),
            in_specs=[pl.BlockSpec(memory_space=pl.ANY)] * 6,
            out_specs=tuple([pl.BlockSpec(memory_space=pltpu.VMEM)] * 5),
            scratch_shapes=scratch,
            compiler_params=pltpu.CompilerParams(
                collective_id=0, has_side_effects=True, vmem_limit_bytes=62 * 1024 * 1024
            ),
        )(queries, key_matrix, value_matrix, level_weight, out_weight.reshape(NH * HD, D), grad_out)
        return lay_out(results, T, NH, HD, L, FS)

    return jax.shard_map(
        on_device,
        mesh=mesh,
        in_specs=(
            P("seq", "head", None),
            P("seq", "head", None),
            P("seq", "head", None),
            P(None, "head", "seq"),
            P("head", None, None),
            P("seq", "head"),
        ),
        out_specs=(
            P("seq", "head"),
            P("seq", "head", None),
            P("seq", "head", None),
            P("seq", "head", None),
            P(None, "head", "seq"),
        ),
        check_vma=False,
    )
```

```python
import math

import jax
import jax.numpy as jnp
from jax import lax
from jax.experimental import pallas as pl
from jax.experimental.pallas import tpu as pltpu
from jax.sharding import PartitionSpec as P

F32 = jnp.float32
BF16 = jnp.bfloat16
TILE = 128
CHUNKS = 2


def nn(a, b):
    return jnp.dot(a, b, preferred_element_type=F32)


def nt(a, b):
    return lax.dot_general(a, b, (((1,), (1,)), ((), ())), preferred_element_type=F32)


def make_kernel(T, NH, HD, L, D, FS, n_seq, n_head):
    far = n_seq.bit_length() - 1
    near = L - far
    nx = n_head // 2
    nb = T // TILE
    H = T // 2
    R = T // CHUNKS
    tile_levels = TILE.bit_length()
    c = [2.0 ** (-max(l - 1, 0) / 2) / math.sqrt(HD) for l in range(L)]
    n_sems = 1 + 2 * (nx - 1) * CHUNKS + far + far * (2 * far) + (nx - 1) * CHUNKS * 2 + 1

    def kernel(q_hbm, k_hbm, v_hbm, lw_hbm, w_hbm, g_hbm,
               mo, dq, dk, dv, gl,
               q, k, v, lw, w, gall, vt, qt, lev, at, mix, ds, att_t, att, acc,
               dot_, do, s_send, s_recv, s_pend, f_t, f_n, p_send, p_recv, p_pend,
               p_done, dkl, dvl, sib_send, sib_recv, x_send, x_recv, own,
               raw, ssem, rsem, lsem):
        sid = lax.axis_index("seq")
        hid = lax.axis_index("head")
        chip = lax.div(hid, 2)
        core = lax.rem(hid, 2)
        other = 1 - core
        sib = {"head": chip * 2 + other}

        def chip_at(d):
            return lax.rem(chip + d, nx)

        def chip_from(d):
            return lax.rem(chip + nx - d, nx)

        def bit(b):
            return lax.rem(lax.div(sid, 2**b), 2)

        def seq_peer(b):
            return {"seq": sid + 2**b * (1 - 2 * bit(b))}

        x_to = [None] + [{"head": chip_at(d) * 2 + core} for d in range(1, nx)]
        peers = [sib] + [seq_peer(b) for b in range(far)]

        used = [0]

        def remote(src, dst, dev):
            i = used[0]
            used[0] += 1
            return pltpu.make_async_remote_copy(
                src_ref=src, dst_ref=dst, send_sem=ssem.at[i], recv_sem=rsem.at[i],
                device_id=dev, device_id_type=pl.DeviceIdType.MESH,
            )

        loads = [
            pltpu.make_async_copy(a, b, lsem.at[i])
            for i, (a, b) in enumerate(
                [(k_hbm, raw.at[0]), (v_hbm, raw.at[1]), (lw_hbm, lw), (g_hbm, gall.at[0]), (w_hbm, w), (q_hbm, raw.at[0])]
            )
        ]
        for copy in loads[:-1]:
            copy.start()

        barrier = pltpu.get_barrier_semaphore()
        for dev in peers + x_to[1:]:
            pl.semaphore_signal(barrier, inc=1, device_id=dev, device_id_type=pl.DeviceIdType.MESH)
        pl.semaphore_wait(barrier, len(peers) + nx - 1)

        ag_x = {}
        for part in range(CHUNKS):
            rows = pl.ds(part * R, R)
            for d in range(1, nx):
                ag_x[d, part] = remote(g_hbm.at[rows], gall.at[2 * d, rows], x_to[d])
                ag_x[d, part].start()
        ag_sib = remote(g_hbm, gall.at[1], sib)
        ag_sib.start()

        def by_head(slot, dst):
            def body(i, _):
                rows = pl.ds(pl.multiple_of(i * TILE, TILE), TILE)
                dst[:, rows, :] = jnp.swapaxes(raw[slot, rows], 0, 1)
                return 0

            lax.fori_loop(0, T // TILE, body, 0)

        loads[0].wait()
        by_head(0, k)
        loads[5].start()
        loads[1].wait()
        by_head(1, v)

        def outer(h, _):
            turned = v[h].T
            vt[h] = turned
            state = nn(turned, k[h])
            s_pend[h] = state
            s_send[0, h] = state.astype(BF16)
            return 0

        lax.fori_loop(0, NH, outer, 0)
        s_copy = []
        s_copy.append(remote(s_send.at[0], s_recv.at[0], seq_peer(0)))
        s_copy[0].start()

        rows_i = lax.broadcasted_iota(jnp.int32, (TILE, TILE), 0)
        cols_i = lax.broadcasted_iota(jnp.int32, (TILE, TILE), 1)
        gap = jnp.zeros((TILE, TILE), jnp.int32)
        for e in range(tile_levels - 1):
            gap = gap + (jnp.bitwise_xor(rows_i, cols_i) >= 2**e).astype(jnp.int32)
        lev[...] = jnp.where(rows_i <= cols_i, gap, -1)

        def blank(h, _):
            for bj in range(nb):
                for bi in range(bj):
                    at[h, pl.ds(bj * TILE, TILE), pl.ds(bi * TILE, TILE)] = jnp.zeros((TILE, TILE), BF16)
            return 0

        lax.fori_loop(0, NH, blank, 0)
        for bj in range(nb):
            for bi in range(bj):
                ds[pl.ds(bj * TILE, TILE), pl.ds(bi * TILE, TILE)] = jnp.zeros((TILE, TILE), BF16)
        loads[2].wait()
        loads[5].wait()
        by_head(0, q)

        def weight(l, h):
            return lw[l, pl.ds(h, 1), :] * c[l]

        def block(b):
            return slice(b * TILE, (b + 1) * TILE)

        def tile_of(top, bottom, bj, bi):
            if bj * TILE < H:
                return top[block(bj), block(bi)]
            return bottom[bj * TILE - H:(bj + 1) * TILE - H, bi * TILE - H:(bi + 1) * TILE - H]

        def level_of(bj, bi):
            return (bj ^ bi).bit_length() + tile_levels - 1

        def forward(h, _):
            kh, qh = k[h], q[h]
            qt[h] = qh.T
            top = nt(kh[:H], qh)
            bottom = nt(kh[H:], qh[H:])
            ws = [weight(l, h) for l in range(near)]
            for bi in range(nb):
                m = jnp.zeros((TILE, TILE), F32)
                for l in range(tile_levels):
                    m = jnp.where(lev[...] == l, ws[l][:, block(bi)], m)
                mix[h, bi] = m
                for bj in range(bi + 1):
                    t = tile_of(top, bottom, bj, bi)
                    factor = m if bi == bj else ws[level_of(bj, bi)][:, block(bi)]
                    at[h, pl.ds(bj * TILE, TILE), pl.ds(bi * TILE, TILE)] = (t * factor).astype(BF16)
            vth = vt[h]
            att_t[h, :, :H] = nn(vth[:, :H], at[h, :H, :H])
            att_t[h, :, H:] = nn(vth, at[h, :, H:])
            return 0

        def take_state(b):
            s_copy[b].wait()
            keep = bit(b).astype(F32)

            def body(h, _):
                got = s_recv[b, h].astype(F32)
                f = got * keep
                f_t[b, h] = f.astype(BF16)
                f_n[b, h] = f.T.astype(BF16)
                if b + 1 < far:
                    total = s_pend[h] + got
                    s_pend[h] = total
                    s_send[b + 1, h] = total.astype(BF16)
                return 0

            lax.fori_loop(0, NH, body, 0)
            if b + 1 < far:
                s_copy.append(remote(s_send.at[b + 1], s_recv.at[b + 1], seq_peer(b + 1)))
                s_copy[b + 1].start()

        fwd_copy = {}

        def pass_on(part):
            rows = pl.ds(part * R, R)
            for d in range(1, nx):
                ag_x[d, part].wait_recv()
                fwd_copy[d, part] = remote(gall.at[2 * d, rows], gall.at[2 * d + 1, rows], sib)
                fwd_copy[d, part].start()

        lax.fori_loop(0, NH // 2, forward, 0)
        take_state(0)
        lax.fori_loop(NH // 2, NH, forward, 0)
        for b in range(1, far - 1):
            take_state(b)
        pass_on(0)
        loads[3].wait()
        loads[4].wait()

        MB = min(512, NH * HD)

        def add_mix(slot, src, part, first, last):
            cols = pl.ds(pl.multiple_of(src * FS, FS), FS)

            def body(i, _):
                hd = pl.ds(pl.multiple_of(i * MB, MB), MB)
                lanes = pl.ds(part * R, R)
                term = nt(w[hd, cols], gall[slot, part * R:(part + 1) * R])
                if not first:
                    term = term + acc[hd, lanes]
                acc[hd, lanes] = term
                return 0

            lax.fori_loop(0, NH * HD // MB, body, 0)

        for part in range(CHUNKS):
            add_mix(0, hid, part, True, False)
        ag_sib.wait_recv()
        for part in range(CHUNKS):
            add_mix(1, chip * 2 + other, part, False, False)
        for part in range(CHUNKS):
            if part > 0:
                pass_on(part)
            for d in range(1, nx):
                add_mix(2 * d, chip_from(d) * 2 + core, part, False, False)
            for d in range(1, nx):
                fwd_copy[d, part].wait_recv()
                add_mix(2 * d + 1, chip_from(d) * 2 + other, part, False, False)

        def mix_grad(h, _):
            turned = acc[pl.ds(pl.multiple_of(h * HD, HD), HD), :]
            dot_[h] = turned.astype(BF16)
            do[h] = turned.T.astype(BF16)
            return 0

        lax.fori_loop(0, NH, mix_grad, 0)
        slots = [0]

        def start_chain(j):
            plan, count = [], NH
            for b in range(j):
                split = count % 2 == 0
                plan.append((b, "sum", split))
                count = count // 2 if split else count
            plan.append((j, "last", False))
            plan += [(b, "join", True) for b, _, split in reversed(plan[:-1]) if split]
            return {"level": j, "plan": plan, "at": 0, "offset": sid * 0, "count": NH}

        def send(chain):
            j = chain["level"]
            b, kind, split = chain["plan"][chain["at"]]
            offset, count = chain["offset"], chain["count"]
            if kind == "join":
                part = pl.ds(offset, count)
                copy = remote(p_done.at[j, part], p_done.at[j, part], seq_peer(b))
            else:
                half = count // 2 if split else count
                first = offset + (1 - bit(b)) * half if split else offset
                slot = slots[0]
                slots[0] += half

                def fill(i, _):
                    p_send[slot + i] = p_pend[j, first + i].astype(BF16)
                    return 0

                lax.fori_loop(0, half, fill, 0)
                source = p_send.at[pl.ds(slot, half)]
                if kind == "last":
                    copy = remote(source, p_done.at[j, pl.ds(offset, count)], seq_peer(b))
                else:
                    copy = remote(source, p_recv.at[pl.ds(slot, half)], seq_peer(b))
                    chain["offset"] = offset + bit(b) * half if split else offset
                    chain["count"] = half
                    chain["slot"] = slot
            copy.start()
            chain["copy"] = copy

        def advance(chain):
            j = chain["level"]
            b, kind, split = chain["plan"][chain["at"]]
            chain["copy"].wait()
            if kind == "sum":
                slot, offset = chain["slot"], chain["offset"]

                def add(i, _):
                    p_pend[j, offset + i] = p_pend[j, offset + i] + p_recv[slot + i].astype(F32)
                    return 0

                lax.fori_loop(0, chain["count"], add, 0)
            elif kind == "join":
                chain["offset"] = chain["offset"] - bit(b) * chain["count"]
                chain["count"] *= 2
            chain["at"] += 1
            if chain["at"] < len(chain["plan"]):
                send(chain)

        chains = []
        for j in reversed(range(far)):

            def back_state(h, _):
                scaled = (qt[h].astype(F32) * weight(near + j, h)).astype(BF16)
                p_pend[j, h] = nn(scaled, do[h])
                return 0

            lax.fori_loop(0, NH, back_state, 0)
            chains.append(start_chain(j))
            send(chains[-1])

        def poll():
            for chain in chains:
                if chain["at"] < len(chain["plan"]):
                    advance(chain)

        if far > 1:
            take_state(far - 1)

        def reads(h, _):
            qth = qt[h].astype(F32)
            left = jnp.concatenate([f_t[b, h] for b in range(far)], axis=1)
            right = jnp.concatenate([(qth * weight(near + b, h)).astype(BF16) for b in range(far)], axis=0)
            total = att_t[h] + nn(left, right)
            att[:, pl.ds(pl.multiple_of(h * HD, HD), HD)] = total.T.astype(BF16)
            return 0

        lax.fori_loop(0, NH, reads, 0)

        NB = min(256, FS)

        def project(dst, slot, dest, part):
            rows = slice(part * R, (part + 1) * R)

            def body(i, _):
                lanes = pl.ds(pl.multiple_of(i * NB, NB), NB)
                cols = pl.ds(pl.multiple_of(dest * FS + i * NB, NB), NB)
                dst[slot, rows, lanes] = nn(att[rows], w[:, cols]).astype(BF16)
                return 0

            lax.fori_loop(0, FS // NB, body, 0)

        sib_copy = {}
        for part in range(CHUNKS):
            rows = pl.ds(part * R, R)
            for d in range(1, nx):
                project(sib_send, d, chip_at(d) * 2 + other, part)
                sib_copy[d, part] = remote(sib_send.at[d, rows], sib_recv.at[d, rows], sib)
                sib_copy[d, part].start()
        poll()
        x_copy = {}
        for part in range(CHUNKS):
            rows = pl.ds(part * R, R)
            for d in range(1, nx):
                project(own, d, chip_at(d) * 2 + core, part)
                sib_copy[d, part].wait_recv()
                x_send[d - 1, rows] = (own[d, rows].astype(F32) + sib_recv[d, rows].astype(F32)).astype(BF16)
                x_copy[d, part] = remote(x_send.at[d - 1, rows], x_recv.at[d - 1, rows], x_to[d])
                x_copy[d, part].start()

        poll()

        def backward(h, _):
            kh, qh, vh = k[h], q[h], v[h]
            doth, doh = dot_[h], do[h]
            s_top = nt(kh[:H], qh)
            s_bottom = nt(kh[H:], qh[H:])
            b_top = nn(vh[:H], doth)
            b_bottom = nn(vh[H:], doth[:, H:])
            ws = [weight(l, h) for l in range(near)]
            sums = [[] for _ in range(near)]
            for bi in range(nb):
                far_sums = {}
                for bj in range(bi + 1):
                    back = tile_of(b_top, b_bottom, bj, bi)
                    product = tile_of(s_top, s_bottom, bj, bi) * back
                    if bi == bj:
                        factor = mix[h, bi]
                        for l in range(tile_levels):
                            sums[l].append(
                                jnp.sum(jnp.where(lev[...] == l, product, 0.0), axis=0, keepdims=True)
                            )
                    else:
                        l = level_of(bj, bi)
                        factor = ws[l][:, block(bi)]
                        far_sums[l] = far_sums[l] + product if l in far_sums else product
                    ds[pl.ds(bj * TILE, TILE), pl.ds(bi * TILE, TILE)] = (back * factor).astype(BF16)
                for l in range(tile_levels, near):
                    if l in far_sums:
                        sums[l].append(jnp.sum(far_sums[l], axis=0, keepdims=True))
                    else:
                        sums[l].append(jnp.zeros((1, TILE), F32))
            for l in range(near):
                gl[l, pl.ds(h, 1), :] = jnp.concatenate(sums[l], axis=1) * c[l]
            dvl[h, :H] = nn(at[h, :H, :], doh)
            dvl[h, H:] = nn(at[h, H:, H:], doh[H:])
            dkl[h, :H] = nn(ds[:H, :], qh)
            dkl[h, H:] = nn(ds[H:, H:], qh[H:])
            kt = kh.T
            dqt = jnp.concatenate([nn(kt[:, :H], ds[:H, :H]), nn(kt, ds[:, H:])], axis=1)
            qth = qt[h].astype(F32)
            for b in range(far):
                u = nn(f_n[b, h], doth)
                gl[near + b, pl.ds(h, 1), :] = jnp.sum(u * qth, axis=0, keepdims=True) * c[near + b]
                dqt = dqt + u * weight(near + b, h)
            dq[h] = dqt.T.astype(BF16)
            return 0

        cuts = [0, (3 * NH) // 8, (6 * NH) // 8, NH]
        lax.fori_loop(cuts[0], cuts[1], backward, 0)
        poll()
        lax.fori_loop(cuts[1], cuts[2], backward, 0)
        poll()
        for part in range(CHUNKS):
            project(sib_send, 0, chip * 2 + other, part)
        last_copy = remote(sib_send.at[0], sib_recv.at[0], sib)
        last_copy.start()
        for part in range(CHUNKS):
            project(own, 0, hid, part)
        lax.fori_loop(cuts[2], cuts[3], backward, 0)
        for _ in range(max(2 * far - 1 - 4, 0)):
            poll()

        def finish(h, _):
            r = sum(p_done[j, h].astype(F32) * (1.0 - bit(j).astype(F32)) for j in range(far)).astype(BF16)
            dk[h] = (dkl[h] + nt(v[h], r)).astype(BF16)
            dv[h] = (dvl[h] + nn(k[h], r)).astype(BF16)
            return 0

        lax.fori_loop(0, NH, finish, 0)
        last_copy.wait()
        for part in range(CHUNKS):
            rows = pl.ds(part * R, R)
            total = own[0, rows].astype(F32) + sib_recv[0, rows].astype(F32)
            for d in range(1, nx):
                x_copy[d, part].wait_recv()
                total = total + x_recv[d - 1, rows].astype(F32)
            mo[rows] = total.astype(BF16)
        ag_sib.wait_send()
        for group in (ag_x, fwd_copy, sib_copy, x_copy):
            for copy in group.values():
                copy.wait_send()

    slots_total = 0
    for j in range(far):
        count = NH
        for _ in range(j):
            count = count // 2 if count % 2 == 0 else count
            slots_total += count
        slots_total += count
    V = pltpu.VMEM
    scratch = [
        V((NH, T, HD), BF16), V((NH, T, HD), BF16), V((NH, T, HD), BF16), V((L, NH, T), F32),
        V((NH * HD, D), BF16), V((n_head, T, FS), BF16),
        V((NH, HD, T), BF16), V((NH, HD, T), BF16), V((TILE, TILE), jnp.int32),
        V((NH, T, T), BF16), V((NH, nb, TILE, TILE), F32), V((T, T), BF16),
        V((NH, HD, T), F32), V((T, NH * HD), BF16), V((NH * HD, T), F32),
        V((NH, HD, T), BF16), V((NH, T, HD), BF16),
        V((far, NH, HD, HD), BF16), V((far, NH, HD, HD), BF16), V((NH, HD, HD), F32),
        V((far, NH, HD, HD), BF16), V((far, NH, HD, HD), BF16),
        V((slots_total, HD, HD), BF16), V((slots_total, HD, HD), BF16), V((far, NH, HD, HD), F32),
        V((far, NH, HD, HD), BF16), V((NH, T, HD), F32), V((NH, T, HD), F32),
        V((nx, T, FS), BF16), V((nx, T, FS), BF16), V((nx - 1, T, FS), BF16), V((nx - 1, T, FS), BF16),
        V((nx, T, FS), BF16), V((2, T, NH, HD), BF16),
        pltpu.SemaphoreType.DMA((n_sems,)), pltpu.SemaphoreType.DMA((n_sems,)),
        pltpu.SemaphoreType.DMA((6,)),
    ]
    return kernel, scratch


def lay_out_kernel(mo, dq, dk, dv, gl, mo_out, dq_out, dk_out, dv_out, gl_out):
    mo_out[...] = mo[...]
    for a, b in ((dq, dq_out), (dk, dk_out), (dv, dv_out)):
        b[...] = jnp.swapaxes(a[...], 0, 1)
    gl_out[...] = gl[...]


def lay_out(results, T, NH, HD, L, FS):
    heads = pl.BlockSpec((NH, TILE, HD), lambda i: (0, i, 0))
    tokens = pl.BlockSpec((TILE, NH, HD), lambda i: (i, 0, 0))
    flat = pl.BlockSpec((TILE, FS), lambda i: (i, 0))
    levels = pl.BlockSpec((L, NH, TILE), lambda i: (0, 0, i))
    return pl.pallas_call(
        lay_out_kernel,
        grid=(T // TILE,),
        out_shape=(
            jax.ShapeDtypeStruct((T, FS), BF16),
            jax.ShapeDtypeStruct((T, NH, HD), BF16),
            jax.ShapeDtypeStruct((T, NH, HD), BF16),
            jax.ShapeDtypeStruct((T, NH, HD), BF16),
            jax.ShapeDtypeStruct((L, NH, T), F32),
        ),
        in_specs=[flat, heads, heads, heads, levels],
        out_specs=(flat, tokens, tokens, tokens, levels),
    )(*results)


def solution(mesh):
    n_seq, n_head = mesh.shape["seq"], mesh.shape["head"]

    def on_device(queries, key_matrix, value_matrix, level_weight, out_weight, grad_out):
        T, NH, HD = queries.shape
        L = level_weight.shape[0]
        D = out_weight.shape[2]
        FS = grad_out.shape[1]
        kernel, scratch = make_kernel(T, NH, HD, L, D, FS, n_seq, n_head)
        results = pl.pallas_call(
            kernel,
            out_shape=(
                jax.ShapeDtypeStruct((T, FS), BF16),
                jax.ShapeDtypeStruct((NH, T, HD), BF16),
                jax.ShapeDtypeStruct((NH, T, HD), BF16),
                jax.ShapeDtypeStruct((NH, T, HD), BF16),
                jax.ShapeDtypeStruct((L, NH, T), F32),
            ),
            in_specs=[pl.BlockSpec(memory_space=pl.ANY)] * 6,
            out_specs=tuple([pl.BlockSpec(memory_space=pltpu.VMEM)] * 5),
            scratch_shapes=scratch,
            compiler_params=pltpu.CompilerParams(
                collective_id=0, has_side_effects=True, vmem_limit_bytes=62 * 1024 * 1024
            ),
        )(queries, key_matrix, value_matrix, level_weight, out_weight.reshape(NH * HD, D), grad_out)
        return lay_out(results, T, NH, HD, L, FS)

    return jax.shard_map(
        on_device,
        mesh=mesh,
        in_specs=(
            P("seq", "head", None),
            P("seq", "head", None),
            P("seq", "head", None),
            P(None, "head", "seq"),
            P("head", None, None),
            P("seq", "head"),
        ),
        out_specs=(
            P("seq", "head"),
            P("seq", "head", None),
            P("seq", "head", None),
            P("seq", "head", None),
            P(None, "head", "seq"),
        ),
        check_vma=False,
    )
```
